32 devices in a mesh: grp: 4 (over z), dev: 8 (over y, x, core).
Axes of the slice: x: 2, y: 2, z: 4, core: 2. Of those that a mesh axis runs over, the one named last changes fastest.
Arguments:
- incident: bfloat16 [128, 128, 128], P(('grp', 'dev')), may hold values from -6 to 6
- tmatrix: bfloat16 [128, 128, 128], P(('grp', 'dev')), may hold values from -0.5 to 0.5
- blocks: bfloat16 [4096, 128, 128], P(('grp', 'dev')), may hold values from -0.09375 to 0.09375
- need: int32 [32, 8, 4], P(('grp', 'dev')), may hold values from 0 to 3, as said below
- pair_src: int32 [32, 512], P(('grp', 'dev')), may hold values from 0 to 31
- pair_tgt: int32 [32, 512], P(('grp', 'dev')), may hold values from 0 to 3
- pair_blk: int32 [32, 512], P(('grp', 'dev')), may hold values from 0 to 127
- pair_count: int32 [32], P(('grp', 'dev')), may hold values from 128 to 512, as said below
- factor: float32 [128, 2048], P(('grp', 'dev')), may hold values from -12 to 12
- harmonics: bfloat16 [2048, 128], replicated, may hold values from -0.046875 to 0.046875
- owner: int32 [2048], replicated, may hold values from 0 to 2047, each once
Outputs:
- amplitudes: float32 [2048, 128], P(('grp', 'dev'))
The draws below stay inside these ranges and needn't reach their ends.
Inputs may be any that keep to these rules, and one draw needn't show every extreme that they name: Each row need[k, j] lists 4 distinct local spheres of peer j. `pair_count`: some device has exactly 512 live pairs.
All inputs are finite; a program needn't handle non-finite values.
Results may differ from the reference program's by a relative error of at most 0.0075.
Values may be sent and summed in bfloat16 or wider, within the bound.
A program may use at most 128 MiB of HBM per device.

```python
import jax
import jax.numpy as jnp
from jax import lax

L = 128
Q = 128
NDIR = 2048
SPH_DEV = 4
CAP = 4
NBLK = 128
SWEEPS = 2
PAIR_MAX = 512
DEVS = 32
SPHERES = 128
N_GRP = 4
N_DEV = 8


def draw_need(key, part):
    row_keys = jax.random.split(jax.random.fold_in(key, 11), DEVS * N_DEV)
    shuffled = jax.vmap(lambda row_key: jax.random.permutation(row_key, jnp.arange(SPH_DEV, dtype=jnp.int32)))(row_keys)
    return shuffled[:, :CAP].reshape(DEVS, N_DEV, CAP).astype(jnp.int32)


def draw_pair_count(key, part):
    key_base = jax.random.fold_in(key, 21)
    key_heavy = jax.random.fold_in(key, 22)
    key_busiest = jax.random.fold_in(key, 23)
    drawn = jax.random.randint(key_base, (DEVS,), PAIR_MAX // 4, PAIR_MAX // 2 + 1)
    is_heavy = jax.random.randint(key_heavy, (DEVS,), 0, 16) == 0
    counts = jnp.where(is_heavy, PAIR_MAX, drawn)
    busiest = jax.random.randint(key_busiest, (), 0, DEVS)
    counts = jnp.where(jnp.arange(DEVS) == busiest, PAIR_MAX, counts)
    return counts.astype(jnp.int32)


def set_ends(values, own_key, low, largest):
    extent = values.shape
    place = [jax.random.randint(jax.random.fold_in(own_key, axis), (), 0, extent[axis]) for axis in range(len(extent))]
    values = values.at[tuple(place)].set(low)
    longest = extent.index(max(extent))
    place[longest] = (place[longest] + 1) % extent[longest]
    return values.at[tuple(place)].set(largest)


def strengthened(drawn, own_key, source, target, parts, factor):
    def block_of(dim):
        return (jnp.arange(drawn.shape[dim]) // (drawn.shape[dim] // parts)).reshape((-1,) + (1,) * (drawn.ndim - 1 - dim))

    one_side = jax.random.permutation(own_key, parts)[block_of(target)]
    second = (block_of(target) + parts // 2) % parts
    return jnp.where((block_of(source) == one_side) | (block_of(source) == second), factor * drawn, drawn)


def level_of(stream_key, dims, cuts, low, top_value):
    loudness, own = 1.0, jax.random.fold_in(stream_key, 6)
    for dim, parts in cuts:
        heights = jnp.exp(jax.random.uniform(jax.random.fold_in(own, dim), (parts,), jnp.float32, low / len(cuts), top_value / len(cuts)))
        loudness = loudness * jnp.repeat(heights, dims[dim] // parts).reshape([-1 if axis == dim else 1 for axis in range(len(dims))])
    return loudness


def bell_draw(key, extent, scale, bound, cuts=(), kind=jnp.bfloat16):
    array = scale * jax.random.normal(key, extent, jnp.float32)
    if cuts:
        array = array * level_of(key, extent, cuts, -0.22, 0.18)
    return jnp.clip(array, -bound, bound).astype(kind)


def noise_with(rng, extent, width, most, cuts, heavy, kind=jnp.bfloat16):
    entries = width * jax.random.normal(rng, extent, jnp.float32)
    if cuts:
        entries = entries * level_of(rng, extent, cuts, -0.22, 0.18)
    return jnp.clip(strengthened(entries, jax.random.fold_in(rng, 3), *heavy), -most, most).astype(kind)


def setup_inputs(seed: int = 0) -> dict:
    key_list = jax.random.split(jax.random.key(seed), 12)
    return {
        "incident": bell_draw(key_list[0], (SPHERES, L, Q), 1.0, 6.0, ((0, 32),)),
        "tmatrix": bell_draw(key_list[1], (SPHERES, L, L), L ** -0.5, 0.5, ((0, 32),)),
        "blocks": bell_draw(key_list[2], (DEVS * NBLK, L, L), (L * 32) ** -0.5, 0.09375, ((0, 32),)),
        "need": draw_need(jax.random.fold_in(key_list[11], 71), 0),
        "pair_src": set_ends(jax.random.randint(key_list[4], (DEVS, PAIR_MAX), 0, N_DEV * CAP), jax.random.fold_in(key_list[4], 1), 0, (N_DEV * CAP) - 1).astype(jnp.int32),
        "pair_tgt": set_ends(jax.random.randint(key_list[5], (DEVS, PAIR_MAX), 0, SPH_DEV), jax.random.fold_in(key_list[5], 1), 0, SPH_DEV - 1).astype(jnp.int32),
        "pair_blk": set_ends(jax.random.randint(key_list[6], (DEVS, PAIR_MAX), 0, NBLK), jax.random.fold_in(key_list[6], 1), 0, NBLK - 1).astype(jnp.int32),
        "pair_count": draw_pair_count(jax.random.fold_in(key_list[11], 71), 0),
        "factor": noise_with(key_list[8], (SPHERES, NDIR), 1.0, 12.0, ((0, 32),), (0, 1, 32, 2.75), jnp.float32),
        "harmonics": bell_draw(key_list[9], (NDIR, L), (L * SPHERES) ** -0.5, 0.046875),
        "owner": jax.random.permutation(key_list[10], NDIR).astype(jnp.int32),
    }


def apply_tmatrix(tmatrix, field):
    product = jnp.einsum("skl,slq->skq", tmatrix.astype(jnp.float32), field.astype(jnp.float32), precision=lax.Precision.HIGHEST)
    return lax.optimization_barrier(product.astype(jnp.bfloat16))


def reference(incident, tmatrix, blocks, need, pair_src, pair_tgt, pair_blk, pair_count, factor, harmonics, owner):
    devices_all = N_GRP * N_DEV
    coeff = apply_tmatrix(tmatrix, incident)
    first_dev = (jnp.arange(devices_all, dtype=jnp.int32) // N_DEV) * N_DEV
    peer_ids = first_dev[:, None, None] + jnp.arange(N_DEV, dtype=jnp.int32)[None, :, None]
    global_ids = (peer_ids * SPH_DEV + need).reshape(devices_all, N_DEV * CAP).astype(jnp.int32)
    pair_global = jnp.take_along_axis(global_ids, pair_src, axis=1).astype(jnp.int32)
    blocks_dev = blocks.reshape(devices_all, NBLK, L, L)
    incident_wide = incident.astype(jnp.float32)
    for sweep_index in range(SWEEPS):
        def one_device(packed):
            source_ids, targets, block_ids, count, local_blocks = packed
            source_tiles = jnp.take(coeff, source_ids, axis=0).astype(jnp.float32)
            operators = jnp.take(local_blocks, block_ids, axis=0).astype(jnp.float32)
            contrib = jnp.einsum("pkl,plq->pkq", operators, source_tiles, precision=lax.Precision.HIGHEST)
            pair_live = jnp.arange(PAIR_MAX, dtype=jnp.int32) < count
            selector = ((targets[None, :] == jnp.arange(SPH_DEV, dtype=jnp.int32)[:, None]) & pair_live[None, :]).astype(jnp.float32)
            return jnp.einsum("sp,pkq->skq", selector, contrib, precision=lax.Precision.HIGHEST)

        scattered = lax.map(one_device, (pair_global, pair_tgt, pair_blk, pair_count, blocks_dev))
        scattered = scattered.reshape(SPHERES, L, Q)
        field = (incident_wide + scattered).astype(jnp.bfloat16)
        coeff = apply_tmatrix(tmatrix, field)
    coeff_dev = coeff.reshape(devices_all, SPH_DEV, L, Q)
    factor_dev = factor.reshape(devices_all, SPH_DEV, NDIR)
    table = harmonics.astype(jnp.float32)

    def accumulate(running, packed):
        local_factor, local_coeff = packed
        weighted = lax.optimization_barrier((local_factor[:, :, None] * table[None]).astype(jnp.bfloat16))
        term = jnp.einsum("sdl,slq->dq", weighted.astype(jnp.float32), local_coeff.astype(jnp.float32), precision=lax.Precision.HIGHEST)
        return running + term, None

    far, unused = lax.scan(accumulate, jnp.zeros((NDIR, Q), jnp.float32), (factor_dev, coeff_dev))
    return jnp.take(far, owner, axis=0)
```

```python
import functools

import jax
import jax.numpy as jnp
from jax import lax
from jax.experimental import pallas as pl
from jax.experimental.pallas import tpu as pltpu
from jax.sharding import PartitionSpec as P

SWEEPS = 2
MESH = pl.DeviceIdType.MESH


def bits_for(size):
    return max(1, (size - 1).bit_length())


def flipped(index, mask):
    result = index
    bit = 1
    while bit <= mask:
        if mask & bit:
            result = result + bit * (1 - 2 * ((index // bit) % 2))
        bit *= 2
    return result


def kernel(
    n_grp,
    n_dev,
    count_ref,
    need_ref,
    owner_ref,
    src_ref,
    tgt_ref,
    blk_ref,
    incident_ref,
    tmatrix_ref,
    factor_ref,
    blocks_hbm,
    harmonics_hbm,
    out_ref,
    blocks,
    harmonics,
    sums,
    operator,
    coeffs,
    final,
    table,
    gathered,
    weighted,
    scattered,
    part_send,
    part_recv,
    group_sum,
    z_send,
    z_recv,
    value_col,
    rank_col,
    factor_pad,
    meta,
    meta_smem,
    load_sem,
    send_sem,
    recv_sem,
    z_send_sem,
    z_recv_sem,
):
    grp = lax.axis_index("grp")
    dev = lax.axis_index("dev")
    spheres, rows, cols = incident_ref.shape
    n_blk = blocks.shape[0]
    pairs = src_ref.shape[1]
    slots = n_dev * spheres
    cells = spheres * slots
    n_dir = harmonics.shape[0]
    rows_out = out_ref.shape[0]
    f32 = jnp.float32
    lanes = 128

    barrier = pltpu.get_barrier_semaphore()
    for m in range(1, n_dev):
        pl.semaphore_signal(barrier, inc=1, device_id=(grp, flipped(dev, m)), device_id_type=MESH)
    for m in range(1, n_grp):
        pl.semaphore_signal(barrier, inc=1, device_id=((grp + m) % n_grp, dev), device_id_type=MESH)
    load_blocks = pltpu.make_async_copy(blocks_hbm, blocks, load_sem.at[0])
    load_blocks.start()
    load_harmonics = pltpu.make_async_copy(harmonics_hbm, harmonics, load_sem.at[1])
    load_harmonics.start()

    def gather_copy(sweep, source, target):
        return pltpu.make_async_remote_copy(
            src_ref=coeffs.at[sweep, source],
            dst_ref=coeffs.at[sweep, source],
            send_sem=send_sem.at[sweep, target],
            recv_sem=recv_sem.at[sweep, source],
            device_id=(grp, target),
            device_id_type=MESH,
        )

    def send_coeffs(sweep):
        for m in range(1, n_dev):
            gather_copy(sweep, dev, flipped(dev, m)).start()

    def apply_tmatrix(s, field):
        return jnp.dot(tmatrix_ref[s], field, preferred_element_type=f32).astype(jnp.bfloat16)

    for s in range(spheres):
        coeffs[0, dev, s * rows : (s + 1) * rows, :] = apply_tmatrix(s, incident_ref[s])
    pl.semaphore_wait(barrier, n_dev - 1 + n_grp - 1)
    send_coeffs(0)

    blk_bits, pair_bits = bits_for(n_blk), bits_for(pairs)
    place = lax.broadcasted_iota(jnp.int32, (1, pairs), 1)
    key = jnp.where(place < count_ref[0], tgt_ref[...] * slots + src_ref[...], cells)
    value = (((key << pair_bits) + place) << blk_bits) + blk_ref[...]
    value_col[...] = jnp.transpose(jnp.broadcast_to(value, (lanes, pairs)))
    col = value_col[...]

    def count(hits):
        return jnp.sum(jnp.where(hits, 1, 0), axis=0, keepdims=True)

    rank = jnp.concatenate(
        [count(col < value[:, k : k + lanes]) for k in range(0, pairs, lanes)], axis=1
    )
    rank_col[...] = jnp.transpose(jnp.broadcast_to(rank, (lanes, pairs)))
    key_col = col >> (blk_bits + pair_bits)
    for k in range(0, pairs, lanes):
        spot = lax.broadcasted_iota(jnp.int32, (1, lanes), 1) + k
        hit = rank_col[...] == spot
        ordered = jnp.sum(jnp.where(hit, col, 0), axis=0, keepdims=True)
        meta[0:1, k : k + lanes] = ordered & ((1 << blk_bits) - 1)
        meta[1:2, k : k + lanes] = ordered >> (blk_bits + pair_bits)
    for k in range(0, cells, lanes):
        spot = lax.broadcasted_iota(jnp.int32, (1, lanes), 1) + k
        upto, under = count(key_col <= spot), count(key_col < spot)
        meta[2:3, k : k + lanes] = jnp.where(upto > under, upto - 1, pairs)
    to_smem = pltpu.make_async_copy(meta, meta_smem, load_sem.at[2])
    to_smem.start()
    to_smem.wait()
    load_blocks.wait()

    sums[pairs] = jnp.zeros((rows, rows), jnp.bfloat16)
    step = 4

    def add_blocks(i, total):
        for k in range(step):
            at = i * step + k
            before = jnp.maximum(at - 1, 0)
            keep = jnp.where(meta_smem[1, at] == meta_smem[1, before], 1.0, 0.0)
            block = jnp.clip(meta_smem[0, at], 0, n_blk - 1)
            total = total * keep + blocks[block].astype(f32)
            sums[at] = total.astype(jnp.bfloat16)
        return total

    lax.fori_loop(0, pairs // step, add_blocks, jnp.zeros((rows, rows), f32))

    def place_cells(j, carry):
        for u in range(spheres):
            slot = 0
            for c in range(1, spheres):
                slot = slot + jnp.where(need_ref[0, j, c] == u, c, 0)
            slot = jnp.minimum(slot, spheres - 1)
            for t in range(spheres):
                last = meta_smem[2, t * slots + j * spheres + slot]
                total = sums[jnp.clip(last, 0, pairs)]
                operator[j, t * rows : (t + 1) * rows, u * rows : (u + 1) * rows] = total
        return carry

    lax.fori_loop(0, n_dev, place_cells, 0)

    def sweep_sum(sweep):
        scattered[...] = jnp.dot(operator[dev], coeffs[sweep, dev], preferred_element_type=f32)
        for m in range(1, n_dev):
            peer = flipped(dev, m)
            gather_copy(sweep, peer, dev).wait_recv()
            scattered[...] += jnp.dot(operator[peer], coeffs[sweep, peer], preferred_element_type=f32)

    def field_of(s):
        wide = incident_ref[s].astype(f32) + scattered[s * rows : (s + 1) * rows, :]
        return wide.astype(jnp.bfloat16)

    sweep_sum(0)
    for s in range(spheres):
        coeffs[1, dev, s * rows : (s + 1) * rows, :] = apply_tmatrix(s, field_of(s))
    send_coeffs(1)

    load_harmonics.wait()
    factor_pad[...] = jnp.zeros_like(factor_pad)
    for k in range(0, n_dir, lanes):
        factor_pad[0:spheres, :] = factor_ref[:, k : k + lanes]
        table[k : k + lanes, lanes:] = jnp.transpose(factor_pad[...])
        table[k : k + lanes, :lanes] = harmonics[k : k + lanes, :].astype(f32)
    chunk = n_grp * rows_out
    row_step = 8

    def weigh(p, carry):
        for z in range(n_grp):

            def fetch(i, inner):
                for k in range(row_step):
                    row = i * row_step + k
                    source = owner_ref[(z * n_dev + p) * rows_out + row]
                    gathered[pl.ds(z * rows_out + row, 1), :] = table[pl.ds(source, 1), :]
                return inner

            lax.fori_loop(0, rows_out // row_step, fetch, 0)
        for s in range(spheres):
            phase = gathered[:, lanes + s : lanes + s + 1]
            product = phase * gathered[:, :lanes]
            weighted[p, :, s * lanes : (s + 1) * lanes] = product.astype(jnp.bfloat16)
        return carry

    lax.fori_loop(0, n_dev, weigh, 0)

    sweep_sum(1)
    for s in range(spheres):
        final[s * rows : (s + 1) * rows, :] = apply_tmatrix(s, field_of(s))

    def part_copy(source, target):
        return pltpu.make_async_remote_copy(
            src_ref=part_send.at[target],
            dst_ref=part_recv.at[source],
            send_sem=send_sem.at[SWEEPS, target],
            recv_sem=recv_sem.at[SWEEPS, source],
            device_id=(grp, target),
            device_id_type=MESH,
        )

    for m in range(1, n_dev):
        peer = flipped(dev, m)
        part = jnp.dot(weighted[peer], final[...], preferred_element_type=f32)
        part_send[peer] = part.astype(part_send.dtype)
        part_copy(dev, peer).start()
    group_sum[...] = jnp.dot(weighted[dev], final[...], preferred_element_type=f32)
    for m in range(1, n_dev):
        peer = flipped(dev, m)
        part_copy(peer, dev).wait_recv()
        group_sum[...] += part_recv[peer].astype(f32)

    def z_copy(source, target):
        return pltpu.make_async_remote_copy(
            src_ref=z_send.at[target],
            dst_ref=z_recv.at[source],
            send_sem=z_send_sem.at[target],
            recv_sem=z_recv_sem.at[source],
            device_id=(target, dev),
            device_id_type=MESH,
        )

    for z in range(n_grp):
        z_send[z] = group_sum[z * rows_out : (z + 1) * rows_out, :].astype(z_send.dtype)
    for m in range(1, n_grp):
        z_copy(grp, (grp + m) % n_grp).start()
    start = pl.multiple_of(grp * rows_out, rows_out)
    out_ref[...] = group_sum[pl.ds(start, rows_out), :]
    for m in range(1, n_grp):
        peer = (grp + m) % n_grp
        z_copy(peer, grp).wait_recv()
        out_ref[...] += z_recv[peer].astype(f32)
    for m in range(1, n_grp):
        z_copy(grp, (grp + m) % n_grp).wait_send()
    for m in range(1, n_dev):
        peer = flipped(dev, m)
        for sweep in range(SWEEPS):
            gather_copy(sweep, dev, peer).wait_send()
        part_copy(dev, peer).wait_send()


def body(
    incident,
    tmatrix,
    blocks,
    need,
    pair_src,
    pair_tgt,
    pair_blk,
    pair_count,
    factor,
    harmonics,
    owner,
):
    n_dev = lax.axis_size("dev")
    n_grp = lax.axis_size("grp")
    spheres, rows, cols = incident.shape
    n_blk = blocks.shape[0]
    pairs = pair_src.shape[1]
    n_dir = harmonics.shape[0]
    rows_out = n_dir // (n_grp * n_dev)
    chunk = n_grp * rows_out
    wide = spheres * rows
    bf16, f32 = jnp.bfloat16, jnp.float32
    z_type = bf16 if rows_out % 16 == 0 else f32
    meta_shape = (8, max(pairs, spheres * n_dev * spheres))
    smem = pl.BlockSpec(memory_space=pltpu.SMEM)
    vmem = pl.BlockSpec(memory_space=pltpu.VMEM)
    anywhere = pl.BlockSpec(memory_space=pl.ANY)
    dma = pltpu.SemaphoreType.DMA
    return pl.pallas_call(
        functools.partial(kernel, n_grp, n_dev),
        out_shape=jax.ShapeDtypeStruct((rows_out, cols), f32),
        in_specs=[smem] * 3 + [vmem] * 6 + [anywhere] * 2,
        out_specs=vmem,
        scratch_shapes=[
            pltpu.VMEM(blocks.shape, bf16),
            pltpu.VMEM(harmonics.shape, bf16),
            pltpu.VMEM((pairs + 1, rows, rows), bf16),
            pltpu.VMEM((n_dev, wide, wide), bf16),
            pltpu.VMEM((SWEEPS, n_dev, wide, cols), bf16),
            pltpu.VMEM((wide, cols), bf16),
            pltpu.VMEM((n_dir, 256), f32),
            pltpu.VMEM((chunk, 256), f32),
            pltpu.VMEM((n_dev, chunk, wide), bf16),
            pltpu.VMEM((wide, cols), f32),
            pltpu.VMEM((n_dev, chunk, cols), bf16),
            pltpu.VMEM((n_dev, chunk, cols), bf16),
            pltpu.VMEM((chunk, cols), f32),
            pltpu.VMEM((n_grp, rows_out, cols), z_type),
            pltpu.VMEM((n_grp, rows_out, cols), z_type),
            pltpu.VMEM((pairs, 128), jnp.int32),
            pltpu.VMEM((pairs, 128), jnp.int32),
            pltpu.VMEM((128, 128), f32),
            pltpu.VMEM(meta_shape, jnp.int32),
            pltpu.SMEM(meta_shape, jnp.int32),
            dma((3,)),
            dma((SWEEPS + 1, n_dev)),
            dma((SWEEPS + 1, n_dev)),
            dma((n_grp,)),
            dma((n_grp,)),
        ],
        compiler_params=pltpu.CompilerParams(
            collective_id=0, has_side_effects=True, vmem_limit_bytes=60 * 1024 * 1024
        ),
    )(
        pair_count,
        need,
        owner,
        pair_src,
        pair_tgt,
        pair_blk,
        incident,
        tmatrix,
        factor,
        blocks,
        harmonics,
    )


def solution(mesh):
    return jax.shard_map(
        body,
        mesh=mesh,
        in_specs=(
            P(("grp", "dev"), None, None),
            P(("grp", "dev"), None, None),
            P(("grp", "dev"), None, None),
            P(("grp", "dev"), None, None),
            P(("grp", "dev"), None),
            P(("grp", "dev"), None),
            P(("grp", "dev"), None),
            P(("grp", "dev")),
            P(("grp", "dev"), None),
            P(),
            P(),
        ),
        out_specs=P(("grp", "dev"), None),
        check_vma=False,
    )
```

```python
import functools

import jax
import jax.numpy as jnp
from jax import lax
from jax.experimental import pallas as pl
from jax.experimental.pallas import tpu as pltpu
from jax.sharding import PartitionSpec as P

SWEEPS = 2
MESH = pl.DeviceIdType.MESH


def bits_for(size):
    return max(1, (size - 1).bit_length())


def flipped(index, mask):
    result = index
    bit = 1
    while bit <= mask:
        if mask & bit:
            result = result + bit * (1 - 2 * ((index // bit) % 2))
        bit *= 2
    return result


def kernel(
    n_grp,
    n_dev,
    count_ref,
    owner_ref,
    need_ref,
    src_ref,
    tgt_ref,
    blk_ref,
    incident_ref,
    tmatrix_ref,
    factor_ref,
    blocks_hbm,
    harmonics_hbm,
    out_ref,
    blocks,
    harmonics,
    sums,
    operator,
    coeffs,
    final,
    table,
    gathered,
    weighted,
    scattered,
    part_send,
    part_recv,
    pair_send,
    pair_recv,
    group_sum,
    z_send,
    z_recv,
    value_col,
    rank_col,
    factor_pad,
    meta,
    meta_smem,
    load_sem,
    send_sem,
    recv_sem,
    z_send_sem,
    z_recv_sem,
):
    grp = lax.axis_index("grp")
    dev = lax.axis_index("dev")
    spheres, rows, cols = incident_ref.shape
    n_blk = blocks.shape[0]
    pairs = src_ref.shape[1]
    slots = n_dev * spheres
    cells = spheres * slots
    n_dir = harmonics.shape[0]
    rows_out = out_ref.shape[0]
    f32 = jnp.float32
    lanes = 128

    barrier = pltpu.get_barrier_semaphore()
    for m in range(1, n_dev):
        pl.semaphore_signal(barrier, inc=1, device_id=(grp, flipped(dev, m)), device_id_type=MESH)
    for m in range(1, n_grp):
        pl.semaphore_signal(barrier, inc=1, device_id=((grp + m) % n_grp, dev), device_id_type=MESH)
    load_blocks = pltpu.make_async_copy(blocks_hbm, blocks, load_sem.at[0])
    load_blocks.start()
    load_harmonics = pltpu.make_async_copy(harmonics_hbm, harmonics, load_sem.at[1])
    load_harmonics.start()

    def gather_copy(sweep, source, target, mask):
        return pltpu.make_async_remote_copy(
            src_ref=coeffs.at[sweep, source],
            dst_ref=coeffs.at[sweep, source],
            send_sem=send_sem.at[sweep, mask],
            recv_sem=recv_sem.at[sweep, source],
            device_id=(grp, target),
            device_id_type=MESH,
        )

    sibling = flipped(dev, 1)
    others = list(range(2, n_dev, 2))

    def own_copy(sweep, mask):
        return gather_copy(sweep, dev, flipped(dev, mask), mask)

    def relay_copy(sweep, mask):
        return gather_copy(sweep, flipped(dev, mask), sibling, mask + 1)

    def arrival(sweep, mask):
        return gather_copy(sweep, flipped(dev, mask), dev, mask)

    def send_coeffs(sweep):
        for m in others[::-1] + [1]:
            own_copy(sweep, m).start()

    def relay(sweep):
        for m in others:
            arrival(sweep, m).wait_recv()
            relay_copy(sweep, m).start()

    def apply_tmatrix(s, field):
        return jnp.dot(tmatrix_ref[s], field, preferred_element_type=f32).astype(jnp.bfloat16)

    for s in range(spheres):
        coeffs[0, dev, s * rows : (s + 1) * rows, :] = apply_tmatrix(s, incident_ref[s])
    pl.semaphore_wait(barrier, n_dev - 1 + n_grp - 1)
    send_coeffs(0)

    blk_bits, pair_bits = bits_for(n_blk), bits_for(pairs)
    place = lax.broadcasted_iota(jnp.int32, (1, pairs), 1)
    key = jnp.where(place < count_ref[0], tgt_ref[...] * slots + src_ref[...], cells)
    value = (((key << pair_bits) + place) << blk_bits) + blk_ref[...]
    value_col[...] = jnp.transpose(jnp.broadcast_to(value, (lanes, pairs)))
    col = value_col[...]

    def count(hits):
        return jnp.sum(jnp.where(hits, 1, 0), axis=0, keepdims=True)

    rank = jnp.concatenate(
        [count(col < value[:, k : k + lanes]) for k in range(0, pairs, lanes)], axis=1
    )
    rank_col[...] = jnp.transpose(jnp.broadcast_to(rank, (lanes, pairs)))
    key_col = col >> (blk_bits + pair_bits)
    for k in range(0, pairs, lanes):
        spot = lax.broadcasted_iota(jnp.int32, (1, lanes), 1) + k
        hit = rank_col[...] == spot
        ordered = jnp.sum(jnp.where(hit, col, 0), axis=0, keepdims=True)
        meta[0:1, k : k + lanes] = ordered & ((1 << blk_bits) - 1)
        meta[1:2, k : k + lanes] = ordered >> (blk_bits + pair_bits)
    for k in range(0, cells, lanes):
        spot = lax.broadcasted_iota(jnp.int32, (1, lanes), 1) + k
        upto, under = count(key_col <= spot), count(key_col < spot)
        meta[2:3, k : k + lanes] = jnp.where(upto > under, upto - 1, pairs)
    meta[8 : 8 + n_dev, 0:spheres] = need_ref[0]
    to_smem = pltpu.make_async_copy(meta, meta_smem, load_sem.at[2])
    to_smem.start()
    to_smem.wait()
    load_blocks.wait()

    sums[pairs] = jnp.zeros((rows, rows), jnp.bfloat16)
    step = 4

    def add_blocks(i, total):
        for k in range(step):
            at = i * step + k
            before = jnp.maximum(at - 1, 0)
            keep = jnp.where(meta_smem[1, at] == meta_smem[1, before], 1.0, 0.0)
            block = jnp.clip(meta_smem[0, at], 0, n_blk - 1)
            total = total * keep + blocks[block].astype(f32)
            sums[at] = total.astype(jnp.bfloat16)
        return total

    lax.fori_loop(0, pairs // step, add_blocks, jnp.zeros((rows, rows), f32))

    relay(0)

    def place_cells(j, carry):
        for u in range(spheres):
            slot = 0
            for c in range(1, spheres):
                slot = slot + jnp.where(meta_smem[8 + j, c] == u, c, 0)
            slot = jnp.minimum(slot, spheres - 1)
            for t in range(spheres):
                last = meta_smem[2, t * slots + j * spheres + slot]
                total = sums[jnp.clip(last, 0, pairs)]
                operator[j, t * rows : (t + 1) * rows, u * rows : (u + 1) * rows] = total
        return carry

    lax.fori_loop(0, n_dev, place_cells, 0)

    def sweep_sum(sweep):
        scattered[...] = jnp.dot(operator[dev], coeffs[sweep, dev], preferred_element_type=f32)
        for m in others + [1] + [m + 1 for m in others]:
            peer = flipped(dev, m)
            if m % 2:
                arrival(sweep, m).wait_recv()
            scattered[...] += jnp.dot(operator[peer], coeffs[sweep, peer], preferred_element_type=f32)

    def field_of(s):
        wide = incident_ref[s].astype(f32) + scattered[s * rows : (s + 1) * rows, :]
        return wide.astype(jnp.bfloat16)

    sweep_sum(0)
    for s in range(spheres):
        coeffs[1, dev, s * rows : (s + 1) * rows, :] = apply_tmatrix(s, field_of(s))
    send_coeffs(1)

    load_harmonics.wait()
    factor_pad[...] = jnp.zeros_like(factor_pad)
    for k in range(0, n_dir, lanes):
        factor_pad[0:spheres, :] = factor_ref[:, k : k + lanes]
        table[k : k + lanes, lanes:] = jnp.transpose(factor_pad[...])
        table[k : k + lanes, :lanes] = harmonics[k : k + lanes, :].astype(f32)
    chunk = n_grp * rows_out
    row_step = 8

    def weigh(p, carry):
        for z in range(n_grp):

            def fetch(i, inner):
                for k in range(row_step):
                    row = i * row_step + k
                    source = owner_ref[(z * n_dev + p) * rows_out + row]
                    gathered[pl.ds(z * rows_out + row, 1), :] = table[pl.ds(source, 1), :]
                return inner

            lax.fori_loop(0, rows_out // row_step, fetch, 0)
        for s in range(spheres):
            phase = gathered[:, lanes + s : lanes + s + 1]
            product = phase * gathered[:, :lanes]
            weighted[p, :, s * lanes : (s + 1) * lanes] = product.astype(jnp.bfloat16)
        return carry

    early = n_dev * 5 // 8
    lax.fori_loop(0, early, weigh, 0)
    relay(1)
    lax.fori_loop(early, n_dev, weigh, 0)

    sweep_sum(1)
    for s in range(spheres):
        final[s * rows : (s + 1) * rows, :] = apply_tmatrix(s, field_of(s))

    def part_copy(mask):
        return pltpu.make_async_remote_copy(
            src_ref=part_send.at[mask // 2],
            dst_ref=part_recv.at[mask // 2],
            send_sem=send_sem.at[SWEEPS, mask],
            recv_sem=recv_sem.at[SWEEPS, mask],
            device_id=(grp, flipped(dev, mask)),
            device_id_type=MESH,
        )

    def pair_copy(mask):
        return pltpu.make_async_remote_copy(
            src_ref=pair_send.at[mask // 2],
            dst_ref=pair_recv.at[mask // 2],
            send_sem=send_sem.at[SWEEPS, mask + 1],
            recv_sem=recv_sem.at[SWEEPS, mask + 1],
            device_id=(grp, sibling),
            device_id_type=MESH,
        )

    def part(mask):
        return jnp.dot(weighted[flipped(dev, mask)], final[...], preferred_element_type=f32)

    far_order = others[::-1] + [0]
    for m in far_order:
        pair_send[m // 2] = part(m + 1)
        pair_copy(m).start()
    for m in far_order:
        own = part(m)
        pair_copy(m).wait_recv()
        total = own + pair_recv[m // 2]
        if m:
            part_send[m // 2] = total.astype(part_send.dtype)
            part_copy(m).start()
        else:
            group_sum[...] = total
    for m in others:
        part_copy(m).wait_recv()
        group_sum[...] += part_recv[m // 2].astype(f32)

    def z_copy(source, target):
        return pltpu.make_async_remote_copy(
            src_ref=z_send.at[target],
            dst_ref=z_recv.at[source],
            send_sem=z_send_sem.at[target],
            recv_sem=z_recv_sem.at[source],
            device_id=(target, dev),
            device_id_type=MESH,
        )

    for z in range(n_grp):
        z_send[z] = group_sum[z * rows_out : (z + 1) * rows_out, :].astype(z_send.dtype)
    for m in range(1, n_grp):
        z_copy(grp, (grp + m) % n_grp).start()
    start = pl.multiple_of(grp * rows_out, rows_out)
    out_ref[...] = group_sum[pl.ds(start, rows_out), :]
    for m in range(1, n_grp):
        peer = (grp + m) % n_grp
        z_copy(peer, grp).wait_recv()
        out_ref[...] += z_recv[peer].astype(f32)
    for m in range(1, n_grp):
        z_copy(grp, (grp + m) % n_grp).wait_send()
    for sweep in range(SWEEPS):
        for m in others + [1]:
            own_copy(sweep, m).wait_send()
        for m in others:
            relay_copy(sweep, m).wait_send()
    for m in far_order:
        pair_copy(m).wait_send()
        if m:
            part_copy(m).wait_send()


def body(
    incident,
    tmatrix,
    blocks,
    need,
    pair_src,
    pair_tgt,
    pair_blk,
    pair_count,
    factor,
    harmonics,
    owner,
):
    n_dev = lax.axis_size("dev")
    n_grp = lax.axis_size("grp")
    spheres, rows, cols = incident.shape
    n_blk = blocks.shape[0]
    pairs = pair_src.shape[1]
    n_dir = harmonics.shape[0]
    rows_out = n_dir // (n_grp * n_dev)
    chunk = n_grp * rows_out
    wide = spheres * rows
    bf16, f32 = jnp.bfloat16, jnp.float32
    z_type = bf16 if rows_out % 16 == 0 else f32
    meta_shape = (8 + (n_dev + 7) // 8 * 8, max(pairs, spheres * n_dev * spheres))
    smem = pl.BlockSpec(memory_space=pltpu.SMEM)
    vmem = pl.BlockSpec(memory_space=pltpu.VMEM)
    anywhere = pl.BlockSpec(memory_space=pl.ANY)
    dma = pltpu.SemaphoreType.DMA
    return pl.pallas_call(
        functools.partial(kernel, n_grp, n_dev),
        out_shape=jax.ShapeDtypeStruct((rows_out, cols), f32),
        in_specs=[smem] * 2 + [vmem] * 7 + [anywhere] * 2,
        out_specs=vmem,
        scratch_shapes=[
            pltpu.VMEM(blocks.shape, bf16),
            pltpu.VMEM(harmonics.shape, bf16),
            pltpu.VMEM((pairs + 1, rows, rows), bf16),
            pltpu.VMEM((n_dev, wide, wide), bf16),
            pltpu.VMEM((SWEEPS, n_dev, wide, cols), bf16),
            pltpu.VMEM((wide, cols), bf16),
            pltpu.VMEM((n_dir, 256), f32),
            pltpu.VMEM((chunk, 256), f32),
            pltpu.VMEM((n_dev, chunk, wide), bf16),
            pltpu.VMEM((wide, cols), f32),
            pltpu.VMEM((n_dev // 2, chunk, cols), bf16),
            pltpu.VMEM((n_dev // 2, chunk, cols), bf16),
            pltpu.VMEM((n_dev // 2, chunk, cols), f32),
            pltpu.VMEM((n_dev // 2, chunk, cols), f32),
            pltpu.VMEM((chunk, cols), f32),
            pltpu.VMEM((n_grp, rows_out, cols), z_type),
            pltpu.VMEM((n_grp, rows_out, cols), z_type),
            pltpu.VMEM((pairs, 128), jnp.int32),
            pltpu.VMEM((pairs, 128), jnp.int32),
            pltpu.VMEM((128, 128), f32),
            pltpu.VMEM(meta_shape, jnp.int32),
            pltpu.SMEM(meta_shape, jnp.int32),
            dma((3,)),
            dma((SWEEPS + 1, n_dev)),
            dma((SWEEPS + 1, n_dev)),
            dma((n_grp,)),
            dma((n_grp,)),
        ],
        compiler_params=pltpu.CompilerParams(
            collective_id=0, has_side_effects=True, vmem_limit_bytes=60 * 1024 * 1024
        ),
    )(
        pair_count,
        owner,
        need,
        pair_src,
        pair_tgt,
        pair_blk,
        incident,
        tmatrix,
        factor,
        blocks,
        harmonics,
    )


def solution(mesh):
    return jax.shard_map(
        body,
        mesh=mesh,
        in_specs=(
            P(("grp", "dev"), None, None),
            P(("grp", "dev"), None, None),
            P(("grp", "dev"), None, None),
            P(("grp", "dev"), None, None),
            P(("grp", "dev"), None),
            P(("grp", "dev"), None),
            P(("grp", "dev"), None),
            P(("grp", "dev")),
            P(("grp", "dev"), None),
            P(),
            P(),
        ),
        out_specs=P(("grp", "dev"), None),
        check_vma=False,
    )
```

```python
import functools

import jax
import jax.numpy as jnp
from jax import lax
from jax.experimental import pallas as pl
from jax.experimental.pallas import tpu as pltpu
from jax.sharding import PartitionSpec as P

SWEEPS = 2
MESH = pl.DeviceIdType.MESH


def bits_for(size):
    return max(1, (size - 1).bit_length())


def flipped(index, mask):
    result = index
    bit = 1
    while bit <= mask:
        if mask & bit:
            result = result + bit * (1 - 2 * ((index // bit) % 2))
        bit *= 2
    return result


def kernel(
    n_grp,
    n_dev,
    count_ref,
    owner_ref,
    need_ref,
    src_ref,
    tgt_ref,
    blk_ref,
    incident_ref,
    tmatrix_ref,
    factor_ref,
    blocks_hbm,
    harmonics_hbm,
    out_ref,
    blocks,
    harmonics,
    sums,
    operator,
    coeffs,
    final,
    table,
    gathered,
    weighted,
    scattered,
    part_send,
    part_recv,
    pair_send,
    pair_recv,
    group_sum,
    z_send,
    z_recv,
    value_col,
    rank_col,
    factor_pad,
    meta,
    meta_smem,
    load_sem,
    send_sem,
    recv_sem,
    z_send_sem,
    z_recv_sem,
):
    grp = lax.axis_index("grp")
    dev = lax.axis_index("dev")
    spheres, rows, cols = incident_ref.shape
    n_blk = blocks.shape[0]
    pairs = src_ref.shape[1]
    slots = n_dev * spheres
    cells = spheres * slots
    n_dir = harmonics.shape[0]
    rows_out = out_ref.shape[0]
    f32 = jnp.float32
    lanes = 128

    barrier = pltpu.get_barrier_semaphore()
    for m in range(1, n_dev):
        pl.semaphore_signal(barrier, inc=1, device_id=(grp, flipped(dev, m)), device_id_type=MESH)
    for m in range(1, n_grp):
        pl.semaphore_signal(barrier, inc=1, device_id=((grp + m) % n_grp, dev), device_id_type=MESH)
    load_blocks = pltpu.make_async_copy(blocks_hbm, blocks, load_sem.at[0])
    load_blocks.start()
    load_harmonics = pltpu.make_async_copy(harmonics_hbm, harmonics, load_sem.at[1])
    load_harmonics.start()

    def gather_copy(sweep, source, target, mask):
        return pltpu.make_async_remote_copy(
            src_ref=coeffs.at[sweep, source],
            dst_ref=coeffs.at[sweep, source],
            send_sem=send_sem.at[sweep, mask],
            recv_sem=recv_sem.at[sweep, source],
            device_id=(grp, target),
            device_id_type=MESH,
        )

    sibling = flipped(dev, 1)
    others = list(range(2, n_dev, 2))

    def own_copy(sweep, mask):
        return gather_copy(sweep, dev, flipped(dev, mask), mask)

    def relay_copy(sweep, mask):
        return gather_copy(sweep, flipped(dev, mask), sibling, mask + 1)

    def arrival(sweep, mask):
        return gather_copy(sweep, flipped(dev, mask), dev, mask)

    def send_coeffs(sweep):
        for m in others[::-1] + [1]:
            own_copy(sweep, m).start()

    def relay(sweep):
        for m in others:
            arrival(sweep, m).wait_recv()
            relay_copy(sweep, m).start()

    def apply_tmatrix(s, field):
        return jnp.dot(tmatrix_ref[s], field, preferred_element_type=f32).astype(jnp.bfloat16)

    for s in range(spheres):
        coeffs[0, dev, s * rows : (s + 1) * rows, :] = apply_tmatrix(s, incident_ref[s])
    blk_bits, pair_bits = bits_for(n_blk), bits_for(pairs)
    place = lax.broadcasted_iota(jnp.int32, (1, pairs), 1)
    key = jnp.where(place < count_ref[0], tgt_ref[...] * slots + src_ref[...], cells)
    value = (((key << pair_bits) + place) << blk_bits) + blk_ref[...]
    value_col[...] = jnp.transpose(jnp.broadcast_to(value, (lanes, pairs)))
    col = value_col[...]

    def count(hits):
        return jnp.sum(jnp.where(hits, 1, 0), axis=0, keepdims=True)

    rank = jnp.concatenate(
        [count(col < value[:, k : k + lanes]) for k in range(0, pairs, lanes)], axis=1
    )
    rank_col[...] = jnp.transpose(jnp.broadcast_to(rank, (lanes, pairs)))
    key_col = col >> (blk_bits + pair_bits)
    for k in range(0, pairs, lanes):
        spot = lax.broadcasted_iota(jnp.int32, (1, lanes), 1) + k
        hit = rank_col[...] == spot
        ordered = jnp.sum(jnp.where(hit, col, 0), axis=0, keepdims=True)
        meta[0:1, k : k + lanes] = ordered & ((1 << blk_bits) - 1)
        meta[1:2, k : k + lanes] = ordered >> (blk_bits + pair_bits)
    for k in range(0, cells, lanes):
        spot = lax.broadcasted_iota(jnp.int32, (1, lanes), 1) + k
        upto, under = count(key_col <= spot), count(key_col < spot)
        meta[2:3, k : k + lanes] = jnp.where(upto > under, upto - 1, pairs)
    meta[8 : 8 + spheres, 0:n_dev] = need_ref[0]
    to_smem = pltpu.make_async_copy(meta, meta_smem, load_sem.at[2])
    to_smem.start()
    pl.semaphore_wait(barrier, n_dev - 1 + n_grp - 1)
    send_coeffs(0)
    to_smem.wait()
    load_blocks.wait()

    sums[pairs] = jnp.zeros((rows, rows), jnp.bfloat16)
    step = 16

    def add_blocks(i, total):
        for k in range(step):
            at = i * step + k
            before = jnp.maximum(at - 1, 0)
            keep = jnp.where(meta_smem[1, at] == meta_smem[1, before], 1.0, 0.0)
            block = jnp.clip(meta_smem[0, at], 0, n_blk - 1)
            total = total * keep + blocks[block].astype(f32)
            sums[at] = total.astype(jnp.bfloat16)
        return total

    lax.fori_loop(0, pairs // step, add_blocks, jnp.zeros((rows, rows), f32))

    relay(0)

    def place_cells(j, carry):
        for u in range(spheres):
            slot = 0
            for c in range(1, spheres):
                slot = slot + jnp.where(meta_smem[8 + c, j] == u, c, 0)
            slot = jnp.minimum(slot, spheres - 1)
            for t in range(spheres):
                last = meta_smem[2, t * slots + j * spheres + slot]
                total = sums[jnp.clip(last, 0, pairs)]
                operator[j, t * rows : (t + 1) * rows, u * rows : (u + 1) * rows] = total
        return carry

    lax.fori_loop(0, n_dev, place_cells, 0)

    def sweep_sum(sweep):
        scattered[...] = jnp.dot(operator[dev], coeffs[sweep, dev], preferred_element_type=f32)
        for m in others + [1] + [m + 1 for m in others]:
            peer = flipped(dev, m)
            if m % 2:
                arrival(sweep, m).wait_recv()
            scattered[...] += jnp.dot(operator[peer], coeffs[sweep, peer], preferred_element_type=f32)

    def field_of(s):
        wide = incident_ref[s].astype(f32) + scattered[s * rows : (s + 1) * rows, :]
        return wide.astype(jnp.bfloat16)

    sweep_sum(0)
    for s in range(spheres):
        coeffs[1, dev, s * rows : (s + 1) * rows, :] = apply_tmatrix(s, field_of(s))
    send_coeffs(1)

    load_harmonics.wait()
    factor_pad[...] = jnp.zeros_like(factor_pad)
    factor_pad[0:spheres, :] = factor_ref[...]
    for k in range(0, n_dir, lanes):
        table[k : k + lanes, lanes:] = jnp.transpose(factor_pad[:, k : k + lanes])
        table[k : k + lanes, :lanes] = harmonics[k : k + lanes, :].astype(f32)
    chunk = n_grp * rows_out
    row_step = min(16, rows_out)

    def weigh(p, carry):
        for z in range(n_grp):

            def fetch(i, inner):
                for k in range(row_step):
                    row = i * row_step + k
                    source = owner_ref[(z * n_dev + p) * rows_out + row]
                    gathered[pl.ds(z * rows_out + row, 1), :] = table[pl.ds(source, 1), :]
                return inner

            lax.fori_loop(0, rows_out // row_step, fetch, 0)
        for s in range(spheres):
            phase = gathered[:, lanes + s : lanes + s + 1]
            product = phase * gathered[:, :lanes]
            weighted[p, :, s * lanes : (s + 1) * lanes] = product.astype(jnp.bfloat16)
        return carry

    early = n_dev * 5 // 8
    lax.fori_loop(0, early, weigh, 0)
    relay(1)
    lax.fori_loop(early, n_dev, weigh, 0)

    sweep_sum(1)
    for s in range(spheres):
        final[s * rows : (s + 1) * rows, :] = apply_tmatrix(s, field_of(s))

    def part_copy(mask):
        return pltpu.make_async_remote_copy(
            src_ref=part_send.at[mask // 2],
            dst_ref=part_recv.at[mask // 2],
            send_sem=send_sem.at[SWEEPS, mask],
            recv_sem=recv_sem.at[SWEEPS, mask],
            device_id=(grp, flipped(dev, mask)),
            device_id_type=MESH,
        )

    def pair_copy(mask):
        return pltpu.make_async_remote_copy(
            src_ref=pair_send.at[mask // 2],
            dst_ref=pair_recv.at[mask // 2],
            send_sem=send_sem.at[SWEEPS, mask + 1],
            recv_sem=recv_sem.at[SWEEPS, mask + 1],
            device_id=(grp, sibling),
            device_id_type=MESH,
        )

    def part(mask):
        return jnp.dot(weighted[flipped(dev, mask)], final[...], preferred_element_type=f32)

    far_order = others[::-1] + [0]
    for m in far_order:
        pair_send[m // 2] = part(m + 1)
        pair_copy(m).start()
    for m in far_order:
        own = part(m)
        pair_copy(m).wait_recv()
        total = own + pair_recv[m // 2]
        if m:
            part_send[m // 2] = total.astype(part_send.dtype)
            part_copy(m).start()
        else:
            group_sum[...] = total
    for m in others:
        part_copy(m).wait_recv()
        group_sum[...] += part_recv[m // 2].astype(f32)

    def z_copy(source, target):
        return pltpu.make_async_remote_copy(
            src_ref=z_send.at[target],
            dst_ref=z_recv.at[source],
            send_sem=z_send_sem.at[target],
            recv_sem=z_recv_sem.at[source],
            device_id=(target, dev),
            device_id_type=MESH,
        )

    for z in range(n_grp):
        z_send[z] = group_sum[z * rows_out : (z + 1) * rows_out, :].astype(z_send.dtype)
    for m in range(1, n_grp):
        z_copy(grp, (grp + m) % n_grp).start()
    start = pl.multiple_of(grp * rows_out, rows_out)
    out_ref[...] = group_sum[pl.ds(start, rows_out), :]
    for m in range(1, n_grp):
        peer = (grp + m) % n_grp
        z_copy(peer, grp).wait_recv()
        out_ref[...] += z_recv[peer].astype(f32)
    for m in range(1, n_grp):
        z_copy(grp, (grp + m) % n_grp).wait_send()
    for sweep in range(SWEEPS):
        for m in others + [1]:
            own_copy(sweep, m).wait_send()
        for m in others:
            relay_copy(sweep, m).wait_send()
    for m in far_order:
        pair_copy(m).wait_send()
        if m:
            part_copy(m).wait_send()


def body(
    incident,
    tmatrix,
    blocks,
    need,
    pair_src,
    pair_tgt,
    pair_blk,
    pair_count,
    factor,
    harmonics,
    owner,
):
    n_dev = lax.axis_size("dev")
    n_grp = lax.axis_size("grp")
    spheres, rows, cols = incident.shape
    n_blk = blocks.shape[0]
    pairs = pair_src.shape[1]
    n_dir = harmonics.shape[0]
    rows_out = n_dir // (n_grp * n_dev)
    chunk = n_grp * rows_out
    wide = spheres * rows
    bf16, f32 = jnp.bfloat16, jnp.float32
    z_type = bf16 if rows_out % 16 == 0 else f32
    meta_shape = (8 + (spheres + 7) // 8 * 8, max(pairs, spheres * n_dev * spheres))
    smem = pl.BlockSpec(memory_space=pltpu.SMEM)
    vmem = pl.BlockSpec(memory_space=pltpu.VMEM)
    anywhere = pl.BlockSpec(memory_space=pl.ANY)
    dma = pltpu.SemaphoreType.DMA
    return pl.pallas_call(
        functools.partial(kernel, n_grp, n_dev),
        out_shape=jax.ShapeDtypeStruct((rows_out, cols), f32),
        in_specs=[smem] * 2 + [vmem] * 7 + [anywhere] * 2,
        out_specs=vmem,
        scratch_shapes=[
            pltpu.VMEM(blocks.shape, bf16),
            pltpu.VMEM(harmonics.shape, bf16),
            pltpu.VMEM((pairs + 1, rows, rows), bf16),
            pltpu.VMEM((n_dev, wide, wide), bf16),
            pltpu.VMEM((SWEEPS, n_dev, wide, cols), bf16),
            pltpu.VMEM((wide, cols), bf16),
            pltpu.VMEM((n_dir, 256), f32),
            pltpu.VMEM((chunk, 256), f32),
            pltpu.VMEM((n_dev, chunk, wide), bf16),
            pltpu.VMEM((wide, cols), f32),
            pltpu.VMEM((n_dev // 2, chunk, cols), bf16),
            pltpu.VMEM((n_dev // 2, chunk, cols), bf16),
            pltpu.VMEM((n_dev // 2, chunk, cols), f32),
            pltpu.VMEM((n_dev // 2, chunk, cols), f32),
            pltpu.VMEM((chunk, cols), f32),
            pltpu.VMEM((n_grp, rows_out, cols), z_type),
            pltpu.VMEM((n_grp, rows_out, cols), z_type),
            pltpu.VMEM((pairs, 128), jnp.int32),
            pltpu.VMEM((pairs, 128), jnp.int32),
            pltpu.VMEM((128, n_dir), f32),
            pltpu.VMEM(meta_shape, jnp.int32),
            pltpu.SMEM(meta_shape, jnp.int32),
            dma((3,)),
            dma((SWEEPS + 1, n_dev)),
            dma((SWEEPS + 1, n_dev)),
            dma((n_grp,)),
            dma((n_grp,)),
        ],
        compiler_params=pltpu.CompilerParams(
            collective_id=0, has_side_effects=True, vmem_limit_bytes=60 * 1024 * 1024
        ),
    )(
        pair_count,
        owner,
        need.transpose(0, 2, 1),
        pair_src,
        pair_tgt,
        pair_blk,
        incident,
        tmatrix,
        factor,
        blocks,
        harmonics,
    )


def solution(mesh):
    return jax.shard_map(
        body,
        mesh=mesh,
        in_specs=(
            P(("grp", "dev"), None, None),
            P(("grp", "dev"), None, None),
            P(("grp", "dev"), None, None),
            P(("grp", "dev"), None, None),
            P(("grp", "dev"), None),
            P(("grp", "dev"), None),
            P(("grp", "dev"), None),
            P(("grp", "dev")),
            P(("grp", "dev"), None),
            P(),
            P(),
        ),
        out_specs=P(("grp", "dev"), None),
        check_vma=False,
    )
```

```python
import functools

import jax
import jax.numpy as jnp
from jax import lax
from jax.experimental import pallas as pl
from jax.experimental.pallas import tpu as pltpu
from jax.sharding import PartitionSpec as P

SWEEPS = 2
MESH = pl.DeviceIdType.MESH


def bits_for(size):
    return max(1, (size - 1).bit_length())


def flipped(index, mask):
    result = index
    bit = 1
    while bit <= mask:
        if mask & bit:
            result = result + bit * (1 - 2 * ((index // bit) % 2))
        bit *= 2
    return result


def kernel(
    n_grp,
    n_dev,
    count_ref,
    owner_ref,
    need_ref,
    src_ref,
    tgt_ref,
    blk_ref,
    incident_ref,
    tmatrix_ref,
    factor_ref,
    blocks_hbm,
    harmonics_hbm,
    out_ref,
    blocks,
    harmonics,
    sums,
    operator,
    coeffs,
    final,
    table,
    gathered,
    weighted,
    scattered,
    part_send,
    part_recv,
    far,
    pair_recv,
    z_send,
    z_recv,
    value_col,
    rank_col,
    factor_pad,
    meta,
    meta_smem,
    load_sem,
    send_sem,
    recv_sem,
    part_send_sem,
    part_recv_sem,
    z_send_sem,
    z_recv_sem,
):
    grp = lax.axis_index("grp")
    dev = lax.axis_index("dev")
    spheres, rows, cols = incident_ref.shape
    n_blk = blocks.shape[0]
    pairs = src_ref.shape[1]
    slots = n_dev * spheres
    cells = spheres * slots
    n_dir = harmonics.shape[0]
    rows_out = out_ref.shape[0]
    f32 = jnp.float32
    lanes = 128

    barrier = pltpu.get_barrier_semaphore()
    for m in range(1, n_dev):
        pl.semaphore_signal(barrier, inc=1, device_id=(grp, flipped(dev, m)), device_id_type=MESH)
    for m in range(1, n_grp):
        pl.semaphore_signal(barrier, inc=1, device_id=((grp + m) % n_grp, dev), device_id_type=MESH)
    load_blocks = pltpu.make_async_copy(blocks_hbm, blocks, load_sem.at[0])
    load_blocks.start()
    load_harmonics = pltpu.make_async_copy(harmonics_hbm, harmonics, load_sem.at[1])
    load_harmonics.start()

    def gather_copy(sweep, source, target, mask):
        return pltpu.make_async_remote_copy(
            src_ref=coeffs.at[sweep, source],
            dst_ref=coeffs.at[sweep, source],
            send_sem=send_sem.at[sweep, mask],
            recv_sem=recv_sem.at[sweep, source],
            device_id=(grp, target),
            device_id_type=MESH,
        )

    sibling = flipped(dev, 1)
    others = list(range(2, n_dev, 2))

    def own_copy(sweep, mask):
        return gather_copy(sweep, dev, flipped(dev, mask), mask)

    def relay_copy(sweep, mask):
        return gather_copy(sweep, flipped(dev, mask), sibling, mask + 1)

    def arrival(sweep, mask):
        return gather_copy(sweep, flipped(dev, mask), dev, mask)

    def send_coeffs(sweep):
        for m in others[::-1] + [1]:
            own_copy(sweep, m).start()

    def relay(sweep):
        for m in others:
            arrival(sweep, m).wait_recv()
            relay_copy(sweep, m).start()

    def apply_tmatrix(s, field):
        return jnp.dot(tmatrix_ref[s], field, preferred_element_type=f32).astype(jnp.bfloat16)

    blk_bits, pair_bits = bits_for(n_blk), bits_for(pairs)
    place = lax.broadcasted_iota(jnp.int32, (1, pairs), 1)
    key = jnp.where(place < count_ref[0], tgt_ref[...] * slots + src_ref[...], cells)
    value = (((key << pair_bits) + place) << blk_bits) + blk_ref[...]
    value_col[...] = jnp.transpose(jnp.broadcast_to(value, (lanes, pairs)))
    col = value_col[...]

    def count(hits):
        return jnp.sum(jnp.where(hits, 1, 0), axis=0, keepdims=True)

    rank = jnp.concatenate(
        [count(col < value[:, k : k + lanes]) for k in range(0, pairs, lanes)], axis=1
    )
    rank_col[...] = jnp.transpose(jnp.broadcast_to(rank, (lanes, pairs)))
    key_col = col >> (blk_bits + pair_bits)
    for k in range(0, pairs, lanes):
        spot = lax.broadcasted_iota(jnp.int32, (1, lanes), 1) + k
        hit = rank_col[...] == spot
        ordered = jnp.sum(jnp.where(hit, col, 0), axis=0, keepdims=True)
        meta[0:1, k : k + lanes] = ordered & ((1 << blk_bits) - 1)
        meta[1:2, k : k + lanes] = ordered >> (blk_bits + pair_bits)
    for k in range(0, cells, lanes):
        spot = lax.broadcasted_iota(jnp.int32, (1, lanes), 1) + k
        upto, under = count(key_col <= spot), count(key_col < spot)
        meta[2:3, k : k + lanes] = jnp.where(upto > under, upto - 1, pairs)
    meta[8 : 8 + spheres, 0:n_dev] = need_ref[0]
    to_smem = pltpu.make_async_copy(meta, meta_smem, load_sem.at[2])
    to_smem.start()
    for s in range(spheres):
        coeffs[0, dev, s * rows : (s + 1) * rows, :] = apply_tmatrix(s, incident_ref[s])
    pl.semaphore_wait(barrier, n_dev - 1 + n_grp - 1)
    send_coeffs(0)
    to_smem.wait()
    load_blocks.wait()

    sums[pairs] = jnp.zeros((rows, rows), jnp.bfloat16)
    step = 16

    def add_blocks(i, total):
        for k in range(step):
            at = i * step + k
            before = jnp.maximum(at - 1, 0)
            keep = jnp.where(meta_smem[1, at] == meta_smem[1, before], 1.0, 0.0)
            block = jnp.clip(meta_smem[0, at], 0, n_blk - 1)
            total = total * keep + blocks[block].astype(f32)
            sums[at] = total.astype(jnp.bfloat16)
        return total

    lax.fori_loop(0, pairs // step, add_blocks, jnp.zeros((rows, rows), f32))

    relay(0)

    def place_cells(j, carry):
        for u in range(spheres):
            slot = 0
            for c in range(1, spheres):
                slot = slot + jnp.where(meta_smem[8 + c, j] == u, c, 0)
            slot = jnp.minimum(slot, spheres - 1)
            for t in range(spheres):
                last = meta_smem[2, t * slots + j * spheres + slot]
                total = sums[jnp.clip(last, 0, pairs)]
                operator[j, t * rows : (t + 1) * rows, u * rows : (u + 1) * rows] = total
        return carry

    lax.fori_loop(0, n_dev, place_cells, 0)

    def sweep_sum(sweep):
        scattered[...] = jnp.dot(operator[dev], coeffs[sweep, dev], preferred_element_type=f32)
        for m in others + [1] + [m + 1 for m in others]:
            peer = flipped(dev, m)
            if m % 2:
                arrival(sweep, m).wait_recv()
            scattered[...] += jnp.dot(operator[peer], coeffs[sweep, peer], preferred_element_type=f32)

    def field_of(s):
        wide = incident_ref[s].astype(f32) + scattered[s * rows : (s + 1) * rows, :]
        return wide.astype(jnp.bfloat16)

    sweep_sum(0)
    for s in range(spheres):
        coeffs[1, dev, s * rows : (s + 1) * rows, :] = apply_tmatrix(s, field_of(s))
    send_coeffs(1)

    load_harmonics.wait()
    factor_pad[...] = jnp.zeros_like(factor_pad)
    factor_pad[0:spheres, :] = factor_ref[...]
    for k in range(0, n_dir, lanes):
        table[k : k + lanes, lanes:] = jnp.transpose(factor_pad[:, k : k + lanes])
        table[k : k + lanes, :lanes] = harmonics[k : k + lanes, :].astype(f32)
    half = n_dev // 2
    span = n_dev * rows_out
    row_step = min(16, rows_out)

    def weigh(block, carry):
        def fetch(i, inner):
            first = block * lanes + i * row_step
            place = (first % span) // rows_out
            target = (place % half) * 2 + place // half
            base = ((first // span) * n_dev + target) * rows_out + first % rows_out
            for k in range(row_step):
                source = owner_ref[base + k]
                gathered[pl.ds(i * row_step + k, 1), :] = table[pl.ds(source, 1), :]
            return inner

        lax.fori_loop(0, lanes // row_step, fetch, 0)
        there = pl.ds(pl.multiple_of(block * lanes, lanes), lanes)
        for s in range(spheres):
            phase = gathered[:, lanes + s : lanes + s + 1]
            product = phase * gathered[:, :lanes]
            weighted[there, s * lanes : (s + 1) * lanes] = product.astype(jnp.bfloat16)
        return carry

    early = n_dir // lanes * 5 // 8
    lax.fori_loop(0, early, weigh, 0)
    relay(1)
    lax.fori_loop(early, n_dir // lanes, weigh, 0)

    sweep_sum(1)
    for s in range(spheres):
        final[s * rows : (s + 1) * rows, :] = apply_tmatrix(s, field_of(s))

    core, chip = dev % 2, dev // 2

    def pair_copy(turn):
        return pltpu.make_async_remote_copy(
            src_ref=far.at[turn, 1 - core],
            dst_ref=pair_recv.at[turn],
            send_sem=part_send_sem.at[turn, 0],
            recv_sem=part_recv_sem.at[turn, 0],
            device_id=(grp, sibling),
            device_id_type=MESH,
        )

    def part_copy(turn, mask):
        return pltpu.make_async_remote_copy(
            src_ref=part_send.at[turn, flipped(dev, mask) // 2],
            dst_ref=part_recv.at[turn, mask // 2],
            send_sem=part_send_sem.at[turn, mask // 2],
            recv_sem=part_recv_sem.at[turn, mask // 2],
            device_id=(grp, flipped(dev, mask)),
            device_id_type=MESH,
        )

    def z_copy(turn):
        return pltpu.make_async_remote_copy(
            src_ref=z_send.at[turn],
            dst_ref=z_recv.at[turn],
            send_sem=z_send_sem.at[turn],
            recv_sem=z_recv_sem.at[turn],
            device_id=((grp + 1 + turn) % n_grp, dev),
            device_id_type=MESH,
        )

    for turn in range(n_grp):
        z = (grp + 1 + turn) % n_grp
        rows_of = pl.ds(pl.multiple_of(z * span, span), span)
        result = jnp.dot(weighted[rows_of, :], final[...], preferred_element_type=f32)
        for c in range(2):
            far[turn, c] = result[c * half * rows_out : (c + 1) * half * rows_out, :]
        pair_copy(turn).start()
    for turn in range(n_grp):
        pair_copy(turn).wait_recv()
        total = far[turn, core] + pair_recv[turn]
        for h in range(half):
            piece = total[h * rows_out : (h + 1) * rows_out, :]
            part_send[turn, h] = piece.astype(part_send.dtype)
        for m in others[::-1]:
            part_copy(turn, m).start()
    for turn in range(n_grp):
        mine = pl.ds(pl.multiple_of(chip * rows_out, rows_out), rows_out)
        total = far[turn, core, mine, :] + pair_recv[turn, mine, :]
        for m in others:
            part_copy(turn, m).wait_recv()
            total = total + part_recv[turn, m // 2].astype(f32)
        if turn < n_grp - 1:
            z_send[turn] = total.astype(z_send.dtype)
            z_copy(turn).start()
        else:
            out_ref[...] = total
    for turn in range(n_grp - 1):
        z_copy(turn).wait_recv()
        out_ref[...] += z_recv[turn].astype(f32)
    for turn in range(n_grp):
        pair_copy(turn).wait_send()
        for m in others:
            part_copy(turn, m).wait_send()
        if turn < n_grp - 1:
            z_copy(turn).wait_send()
    for sweep in range(SWEEPS):
        for m in others + [1]:
            own_copy(sweep, m).wait_send()
        for m in others:
            relay_copy(sweep, m).wait_send()


def body(
    incident,
    tmatrix,
    blocks,
    need,
    pair_src,
    pair_tgt,
    pair_blk,
    pair_count,
    factor,
    harmonics,
    owner,
):
    n_dev = lax.axis_size("dev")
    n_grp = lax.axis_size("grp")
    spheres, rows, cols = incident.shape
    n_blk = blocks.shape[0]
    pairs = pair_src.shape[1]
    n_dir = harmonics.shape[0]
    rows_out = n_dir // (n_grp * n_dev)
    half = n_dev // 2
    wide = spheres * rows
    bf16, f32 = jnp.bfloat16, jnp.float32
    z_type = bf16 if rows_out % 16 == 0 else f32
    meta_shape = (8 + (spheres + 7) // 8 * 8, max(pairs, spheres * n_dev * spheres))
    smem = pl.BlockSpec(memory_space=pltpu.SMEM)
    vmem = pl.BlockSpec(memory_space=pltpu.VMEM)
    anywhere = pl.BlockSpec(memory_space=pl.ANY)
    dma = pltpu.SemaphoreType.DMA
    return pl.pallas_call(
        functools.partial(kernel, n_grp, n_dev),
        out_shape=jax.ShapeDtypeStruct((rows_out, cols), f32),
        in_specs=[smem] * 2 + [vmem] * 7 + [anywhere] * 2,
        out_specs=vmem,
        scratch_shapes=[
            pltpu.VMEM(blocks.shape, bf16),
            pltpu.VMEM(harmonics.shape, bf16),
            pltpu.VMEM((pairs + 1, rows, rows), bf16),
            pltpu.VMEM((n_dev, wide, wide), bf16),
            pltpu.VMEM((SWEEPS, n_dev, wide, cols), bf16),
            pltpu.VMEM((wide, cols), bf16),
            pltpu.VMEM((n_dir, 256), f32),
            pltpu.VMEM((128, 256), f32),
            pltpu.VMEM((n_dir, wide), bf16),
            pltpu.VMEM((wide, cols), f32),
            pltpu.VMEM((n_grp, half, rows_out, cols), z_type),
            pltpu.VMEM((n_grp, half, rows_out, cols), z_type),
            pltpu.VMEM((n_grp, 2, half * rows_out, cols), f32),
            pltpu.VMEM((n_grp, half * rows_out, cols), f32),
            pltpu.VMEM((n_grp, rows_out, cols), z_type),
            pltpu.VMEM((n_grp, rows_out, cols), z_type),
            pltpu.VMEM((pairs, 128), jnp.int32),
            pltpu.VMEM((pairs, 128), jnp.int32),
            pltpu.VMEM((128, n_dir), f32),
            pltpu.VMEM(meta_shape, jnp.int32),
            pltpu.SMEM(meta_shape, jnp.int32),
            dma((3,)),
            dma((SWEEPS, n_dev)),
            dma((SWEEPS, n_dev)),
            dma((n_grp, half)),
            dma((n_grp, half)),
            dma((n_grp,)),
            dma((n_grp,)),
        ],
        compiler_params=pltpu.CompilerParams(
            collective_id=0, has_side_effects=True, vmem_limit_bytes=60 * 1024 * 1024
        ),
    )(
        pair_count,
        owner,
        need.transpose(0, 2, 1),
        pair_src,
        pair_tgt,
        pair_blk,
        incident,
        tmatrix,
        factor,
        blocks,
        harmonics,
    )


def solution(mesh):
    return jax.shard_map(
        body,
        mesh=mesh,
        in_specs=(
            P(("grp", "dev"), None, None),
            P(("grp", "dev"), None, None),
            P(("grp", "dev"), None, None),
            P(("grp", "dev"), None, None),
            P(("grp", "dev"), None),
            P(("grp", "dev"), None),
            P(("grp", "dev"), None),
            P(("grp", "dev")),
            P(("grp", "dev"), None),
            P(),
            P(),
        ),
        out_specs=P(("grp", "dev"), None),
        check_vma=False,
    )
```

```python
import functools

import jax
import jax.numpy as jnp
from jax import lax
from jax.experimental import pallas as pl
from jax.experimental.pallas import tpu as pltpu
from jax.sharding import PartitionSpec as P

SWEEPS = 2
MESH = pl.DeviceIdType.MESH


def bits_for(size):
    return max(1, (size - 1).bit_length())


def flipped(index, mask):
    result = index
    bit = 1
    while bit <= mask:
        if mask & bit:
            result = result + bit * (1 - 2 * ((index // bit) % 2))
        bit *= 2
    return result


def kernel(
    n_grp,
    n_dev,
    count_ref,
    owner_ref,
    need_ref,
    src_ref,
    tgt_ref,
    blk_ref,
    incident_ref,
    tmatrix_ref,
    factor_ref,
    blocks_hbm,
    harmonics_hbm,
    out_ref,
    blocks,
    harmonics,
    sums,
    operator,
    coeffs,
    final,
    table,
    gathered,
    weighted,
    scattered,
    part_send,
    part_recv,
    far,
    pair_recv,
    z_send,
    z_recv,
    value_col,
    rank_col,
    factor_pad,
    meta,
    meta_smem,
    load_sem,
    send_sem,
    recv_sem,
    part_send_sem,
    part_recv_sem,
    z_send_sem,
    z_recv_sem,
):
    grp = lax.axis_index("grp")
    dev = lax.axis_index("dev")
    spheres, rows, cols = incident_ref.shape
    n_blk = blocks.shape[0]
    pairs = src_ref.shape[1]
    slots = n_dev * spheres
    cells = spheres * slots
    n_dir = harmonics.shape[0]
    rows_out = out_ref.shape[0]
    f32 = jnp.float32
    lanes = 128

    barrier = pltpu.get_barrier_semaphore()
    for m in range(1, n_dev):
        pl.semaphore_signal(barrier, inc=1, device_id=(grp, flipped(dev, m)), device_id_type=MESH)
    for m in range(1, n_grp):
        pl.semaphore_signal(barrier, inc=1, device_id=((grp + m) % n_grp, dev), device_id_type=MESH)
    load_blocks = pltpu.make_async_copy(blocks_hbm, blocks, load_sem.at[0])
    load_blocks.start()
    load_harmonics = pltpu.make_async_copy(harmonics_hbm, harmonics, load_sem.at[1])
    load_harmonics.start()

    def gather_copy(sweep, source, target, mask):
        return pltpu.make_async_remote_copy(
            src_ref=coeffs.at[sweep, source],
            dst_ref=coeffs.at[sweep, source],
            send_sem=send_sem.at[sweep, mask],
            recv_sem=recv_sem.at[sweep, source],
            device_id=(grp, target),
            device_id_type=MESH,
        )

    sibling = flipped(dev, 1)
    others = list(range(2, n_dev, 2))

    def own_copy(sweep, mask):
        return gather_copy(sweep, dev, flipped(dev, mask), mask)

    def relay_copy(sweep, mask):
        return gather_copy(sweep, flipped(dev, mask), sibling, mask + 1)

    def arrival(sweep, mask):
        return gather_copy(sweep, flipped(dev, mask), dev, mask)

    def send_coeffs(sweep):
        for m in others[::-1] + [1]:
            own_copy(sweep, m).start()

    def relay(sweep):
        for m in others:
            arrival(sweep, m).wait_recv()
            relay_copy(sweep, m).start()

    def apply_tmatrix(s, field):
        return jnp.dot(tmatrix_ref[s], field, preferred_element_type=f32).astype(jnp.bfloat16)

    blk_bits, pair_bits = bits_for(n_blk), bits_for(pairs)
    place = lax.broadcasted_iota(jnp.int32, (1, pairs), 1)
    key = jnp.where(place < count_ref[0], tgt_ref[...] * slots + src_ref[...], cells)
    value = (((key << pair_bits) + place) << blk_bits) + blk_ref[...]
    value_col[...] = jnp.transpose(jnp.broadcast_to(value, (lanes, pairs)))
    col = value_col[...]

    def count(hits):
        return jnp.sum(jnp.where(hits, 1, 0), axis=0, keepdims=True)

    rank = jnp.concatenate(
        [count(col < value[:, k : k + lanes]) for k in range(0, pairs, lanes)], axis=1
    )
    rank_col[...] = jnp.transpose(jnp.broadcast_to(rank, (lanes, pairs)))
    key_col = col >> (blk_bits + pair_bits)
    for k in range(0, pairs, lanes):
        spot = lax.broadcasted_iota(jnp.int32, (1, lanes), 1) + k
        hit = rank_col[...] == spot
        ordered = jnp.sum(jnp.where(hit, col, 0), axis=0, keepdims=True)
        meta[0:1, k : k + lanes] = ordered & ((1 << blk_bits) - 1)
        meta[1:2, k : k + lanes] = ordered >> (blk_bits + pair_bits)
    for k in range(0, cells, lanes):
        spot = lax.broadcasted_iota(jnp.int32, (1, lanes), 1) + k
        upto, under = count(key_col <= spot), count(key_col < spot)
        meta[2:3, k : k + lanes] = jnp.where(upto > under, upto - 1, pairs)
    meta[8 : 8 + spheres, 0:n_dev] = need_ref[0]
    to_smem = pltpu.make_async_copy(meta, meta_smem, load_sem.at[2])
    to_smem.start()
    for s in range(spheres):
        coeffs[0, dev, s * rows : (s + 1) * rows, :] = apply_tmatrix(s, incident_ref[s])
    pl.semaphore_wait(barrier, n_dev - 1 + n_grp - 1)
    send_coeffs(0)
    to_smem.wait()
    load_blocks.wait()

    sums[pairs] = jnp.zeros((rows, rows), jnp.bfloat16)
    step = 4

    def add_blocks(i, total):
        held, keeps = [], []
        for k in range(step):
            at = i * step + k
            before = jnp.maximum(at - 1, 0)
            keeps.append(jnp.where(meta_smem[1, at] == meta_smem[1, before], 1.0, 0.0))
            held.append(blocks[jnp.clip(meta_smem[0, at], 0, n_blk - 1)])
        totals = []
        for k in range(step):
            total = total * keeps[k] + held[k].astype(f32)
            totals.append(total.astype(jnp.bfloat16))
        for k in range(step):
            sums[i * step + k] = totals[k]
        return total

    lax.fori_loop(0, pairs // step, add_blocks, jnp.zeros((rows, rows), f32))

    relay(0)

    def place_cells(j, carry):
        for u in range(spheres):
            slot = 0
            for c in range(1, spheres):
                slot = slot + jnp.where(meta_smem[8 + c, j] == u, c, 0)
            slot = jnp.minimum(slot, spheres - 1)
            found = []
            for t in range(spheres):
                last = meta_smem[2, t * slots + j * spheres + slot]
                found.append(sums[jnp.clip(last, 0, pairs)])
            for t in range(spheres):
                operator[j, t * rows : (t + 1) * rows, u * rows : (u + 1) * rows] = found[t]
        return carry

    lax.fori_loop(0, n_dev, place_cells, 0)

    def sweep_sum(sweep):
        scattered[...] = jnp.dot(operator[dev], coeffs[sweep, dev], preferred_element_type=f32)
        for m in others + [1] + [m + 1 for m in others]:
            peer = flipped(dev, m)
            if m % 2:
                arrival(sweep, m).wait_recv()
            scattered[...] += jnp.dot(operator[peer], coeffs[sweep, peer], preferred_element_type=f32)

    def field_of(s):
        wide = incident_ref[s].astype(f32) + scattered[s * rows : (s + 1) * rows, :]
        return wide.astype(jnp.bfloat16)

    sweep_sum(0)
    for s in range(spheres):
        coeffs[1, dev, s * rows : (s + 1) * rows, :] = apply_tmatrix(s, field_of(s))
    send_coeffs(1)

    load_harmonics.wait()
    factor_pad[...] = jnp.zeros_like(factor_pad)
    factor_pad[0:spheres, :] = factor_ref[...]
    for k in range(0, n_dir, lanes):
        table[k : k + lanes, lanes:] = jnp.transpose(factor_pad[:, k : k + lanes])
        table[k : k + lanes, :lanes] = harmonics[k : k + lanes, :].astype(f32)
    half = n_dev // 2
    span = n_dev * rows_out
    row_step = min(16, rows_out)

    def weigh(block, carry):
        def fetch(i, inner):
            first = block * lanes + i * row_step
            place = (first % span) // rows_out
            target = (place % half) * 2 + place // half
            base = ((first // span) * n_dev + target) * rows_out + first % rows_out
            found = [table[pl.ds(owner_ref[base + k], 1), :] for k in range(row_step)]
            for k in range(row_step):
                gathered[pl.ds(i * row_step + k, 1), :] = found[k]
            return inner

        lax.fori_loop(0, lanes // row_step, fetch, 0)
        there = pl.ds(pl.multiple_of(block * lanes, lanes), lanes)
        for s in range(spheres):
            phase = gathered[:, lanes + s : lanes + s + 1]
            product = phase * gathered[:, :lanes]
            weighted[there, s * lanes : (s + 1) * lanes] = product.astype(jnp.bfloat16)
        return carry

    early = n_dir // lanes * 5 // 8
    lax.fori_loop(0, early, weigh, 0)
    relay(1)
    lax.fori_loop(early, n_dir // lanes, weigh, 0)

    sweep_sum(1)
    for s in range(spheres):
        final[s * rows : (s + 1) * rows, :] = apply_tmatrix(s, field_of(s))

    core, chip = dev % 2, dev // 2

    def pair_copy(turn):
        return pltpu.make_async_remote_copy(
            src_ref=far.at[turn, 1 - core],
            dst_ref=pair_recv.at[turn],
            send_sem=part_send_sem.at[turn, 0],
            recv_sem=part_recv_sem.at[turn, 0],
            device_id=(grp, sibling),
            device_id_type=MESH,
        )

    def part_copy(turn, mask):
        return pltpu.make_async_remote_copy(
            src_ref=part_send.at[turn, flipped(dev, mask) // 2],
            dst_ref=part_recv.at[turn, mask // 2],
            send_sem=part_send_sem.at[turn, mask // 2],
            recv_sem=part_recv_sem.at[turn, mask // 2],
            device_id=(grp, flipped(dev, mask)),
            device_id_type=MESH,
        )

    def z_copy(turn):
        return pltpu.make_async_remote_copy(
            src_ref=z_send.at[turn],
            dst_ref=z_recv.at[turn],
            send_sem=z_send_sem.at[turn],
            recv_sem=z_recv_sem.at[turn],
            device_id=((grp + 1 + turn) % n_grp, dev),
            device_id_type=MESH,
        )

    for turn in range(n_grp):
        z = (grp + 1 + turn) % n_grp
        rows_of = pl.ds(pl.multiple_of(z * span, span), span)
        result = jnp.dot(weighted[rows_of, :], final[...], preferred_element_type=f32)
        for c in range(2):
            far[turn, c] = result[c * half * rows_out : (c + 1) * half * rows_out, :]
        pair_copy(turn).start()
    for turn in range(n_grp):
        pair_copy(turn).wait_recv()
        total = far[turn, core] + pair_recv[turn]
        for h in range(half):
            piece = total[h * rows_out : (h + 1) * rows_out, :]
            part_send[turn, h] = piece.astype(part_send.dtype)
        for m in others[::-1]:
            part_copy(turn, m).start()
    for turn in range(n_grp):
        mine = pl.ds(pl.multiple_of(chip * rows_out, rows_out), rows_out)
        total = far[turn, core, mine, :] + pair_recv[turn, mine, :]
        for m in others:
            part_copy(turn, m).wait_recv()
            total = total + part_recv[turn, m // 2].astype(f32)
        if turn < n_grp - 1:
            z_send[turn] = total.astype(z_send.dtype)
            z_copy(turn).start()
        else:
            out_ref[...] = total
    for turn in range(n_grp - 1):
        z_copy(turn).wait_recv()
        out_ref[...] += z_recv[turn].astype(f32)
    for turn in range(n_grp):
        pair_copy(turn).wait_send()
        for m in others:
            part_copy(turn, m).wait_send()
        if turn < n_grp - 1:
            z_copy(turn).wait_send()
    for sweep in range(SWEEPS):
        for m in others + [1]:
            own_copy(sweep, m).wait_send()
        for m in others:
            relay_copy(sweep, m).wait_send()


def body(
    incident,
    tmatrix,
    blocks,
    need,
    pair_src,
    pair_tgt,
    pair_blk,
    pair_count,
    factor,
    harmonics,
    owner,
):
    n_dev = lax.axis_size("dev")
    n_grp = lax.axis_size("grp")
    spheres, rows, cols = incident.shape
    n_blk = blocks.shape[0]
    pairs = pair_src.shape[1]
    n_dir = harmonics.shape[0]
    rows_out = n_dir // (n_grp * n_dev)
    half = n_dev // 2
    wide = spheres * rows
    bf16, f32 = jnp.bfloat16, jnp.float32
    z_type = bf16 if rows_out % 16 == 0 else f32
    meta_shape = (8 + (spheres + 7) // 8 * 8, max(pairs, spheres * n_dev * spheres))
    smem = pl.BlockSpec(memory_space=pltpu.SMEM)
    vmem = pl.BlockSpec(memory_space=pltpu.VMEM)
    anywhere = pl.BlockSpec(memory_space=pl.ANY)
    dma = pltpu.SemaphoreType.DMA
    return pl.pallas_call(
        functools.partial(kernel, n_grp, n_dev),
        out_shape=jax.ShapeDtypeStruct((rows_out, cols), f32),
        in_specs=[smem] * 2 + [vmem] * 7 + [anywhere] * 2,
        out_specs=vmem,
        scratch_shapes=[
            pltpu.VMEM(blocks.shape, bf16),
            pltpu.VMEM(harmonics.shape, bf16),
            pltpu.VMEM((pairs + 1, rows, rows), bf16),
            pltpu.VMEM((n_dev, wide, wide), bf16),
            pltpu.VMEM((SWEEPS, n_dev, wide, cols), bf16),
            pltpu.VMEM((wide, cols), bf16),
            pltpu.VMEM((n_dir, 256), f32),
            pltpu.VMEM((128, 256), f32),
            pltpu.VMEM((n_dir, wide), bf16),
            pltpu.VMEM((wide, cols), f32),
            pltpu.VMEM((n_grp, half, rows_out, cols), z_type),
            pltpu.VMEM((n_grp, half, rows_out, cols), z_type),
            pltpu.VMEM((n_grp, 2, half * rows_out, cols), f32),
            pltpu.VMEM((n_grp, half * rows_out, cols), f32),
            pltpu.VMEM((n_grp, rows_out, cols), z_type),
            pltpu.VMEM((n_grp, rows_out, cols), z_type),
            pltpu.VMEM((pairs, 128), jnp.int32),
            pltpu.VMEM((pairs, 128), jnp.int32),
            pltpu.VMEM((128, n_dir), f32),
            pltpu.VMEM(meta_shape, jnp.int32),
            pltpu.SMEM(meta_shape, jnp.int32),
            dma((3,)),
            dma((SWEEPS, n_dev)),
            dma((SWEEPS, n_dev)),
            dma((n_grp, half)),
            dma((n_grp, half)),
            dma((n_grp,)),
            dma((n_grp,)),
        ],
        compiler_params=pltpu.CompilerParams(
            collective_id=0, has_side_effects=True, vmem_limit_bytes=60 * 1024 * 1024
        ),
    )(
        pair_count,
        owner,
        need.transpose(0, 2, 1),
        pair_src,
        pair_tgt,
        pair_blk,
        incident,
        tmatrix,
        factor,
        blocks,
        harmonics,
    )


def solution(mesh):
    return jax.shard_map(
        body,
        mesh=mesh,
        in_specs=(
            P(("grp", "dev"), None, None),
            P(("grp", "dev"), None, None),
            P(("grp", "dev"), None, None),
            P(("grp", "dev"), None, None),
            P(("grp", "dev"), None),
            P(("grp", "dev"), None),
            P(("grp", "dev"), None),
            P(("grp", "dev")),
            P(("grp", "dev"), None),
            P(),
            P(),
        ),
        out_specs=P(("grp", "dev"), None),
        check_vma=False,
    )
```
